32 devices in a mesh: dp: 2 (over y), ctx: 8 (over z, core), fsdp: 2 (over x).
Axes of the slice: x: 2, y: 2, z: 4, core: 2. Of those that a mesh axis runs over, the one named last changes fastest.
Arguments:
- inputs: bfloat16 [8, 2048, 768], P(('dp', 'fsdp'), 'ctx'), may hold values from -6 to 6
- w_qkv: bfloat16 [768, 2304], P('fsdp'), may hold values from -0.21875 to 0.21875
- w_out: bfloat16 [768, 768], P('fsdp'), may hold values from -1.75 to 1.75
- w_up: bfloat16 [768, 3072], P('fsdp'), may hold values from -0.21875 to 0.21875
- w_down: bfloat16 [3072, 768], P('fsdp'), may hold values from -0.109375 to 0.109375
- ln1_gain: bfloat16 [768], P('fsdp'), may hold values from 0.5 to 1.5
- ln1_bias: bfloat16 [768], P('fsdp'), may hold values from -3 to 3
- q_bias: bfloat16 [768], P('fsdp'), may hold values from -4 to 4
- v_bias: bfloat16 [768], P('fsdp'), may hold values from -0.75 to 0.75
- out_bias: bfloat16 [768], P('fsdp'), may hold values from -4 to 4
- ln2_gain: bfloat16 [768], P('fsdp'), may hold values from 0.5 to 1.5
- ln2_bias: bfloat16 [768], P('fsdp'), may hold values from -3 to 3
- up_bias: bfloat16 [3072], P('fsdp'), may hold values from -6 to 6
- down_bias: bfloat16 [768], P('fsdp'), may hold values from -4 to 4
- cotangent: bfloat16 [8, 2048, 768], P(('dp', 'fsdp'), 'ctx'), may hold values from -6 to 6
Outputs:
- output: bfloat16 [8, 2048, 768], P(('dp', 'fsdp'), 'ctx')
- input_grad: bfloat16 [8, 2048, 768], P(('dp', 'fsdp'), 'ctx')
- w_qkv_grad: float32 [768, 2304], P('fsdp')
- w_out_grad: float32 [768, 768], P('fsdp')
- w_up_grad: float32 [768, 3072], P('fsdp')
- w_down_grad: float32 [3072, 768], P('fsdp')
- ln1_gain_grad: float32 [768], P('fsdp')
- ln1_bias_grad: float32 [768], P('fsdp')
- q_bias_grad: float32 [768], P('fsdp')
- v_bias_grad: float32 [768], P('fsdp')
- out_bias_grad: float32 [768], P('fsdp')
- ln2_gain_grad: float32 [768], P('fsdp')
- ln2_bias_grad: float32 [768], P('fsdp')
- up_bias_grad: float32 [3072], P('fsdp')
- down_bias_grad: float32 [768], P('fsdp')
The draws below stay inside these ranges and needn't reach their ends.
All inputs are finite; a program needn't handle non-finite values.
Results may differ from the reference program's by a relative error of at most 0.018.
Values may be sent and summed in bfloat16 or wider, within the bound.
A program may use at most 192 MiB of HBM per device.

```python
import math
from functools import partial
import jax
import jax.numpy as jnp
from jax import lax

D = 768
H = 12
HD = 64
FF = 3072
LEN = 2048
BATCH = 8


def levels(stream_key, dims, cuts, smallest, high):
    level = 1.0
    for position, blocks in cuts:
        steps = jax.random.uniform(jax.random.fold_in(jax.random.fold_in(stream_key, 6), position), (blocks,), jnp.float32, smallest / len(cuts), high / len(cuts))
        level = level * jnp.repeat(jnp.exp(steps), dims[position] // blocks).reshape((-1,) + (1,) * (len(dims) - 1 - position))
    return level


def noise(key, dims, deviation, most, shards=(), kind=jnp.bfloat16):
    values = deviation * jax.random.normal(key, dims, jnp.float32)
    if shards:
        values = values * levels(key, dims, shards, -0.22, 0.18)
    return jnp.clip(values, -most, most).astype(kind)


def setup_inputs(seed: int = 0) -> dict:
    splits = jax.random.split(jax.random.key(seed), 16)
    inputs = noise(splits[0], (BATCH, LEN, D), 1.0, 6.0, ((0, 4), (1, 8)))
    w_qkv = noise(splits[1], (D, 3 * D), D ** -0.5, 0.21875, ((0, 2),))
    w_out = noise(splits[2], (D, D), (D * 32 // LEN) ** -0.5, 1.75, ((0, 2),))
    w_up = noise(splits[3], (D, FF), D ** -0.5, 0.21875, ((0, 2),))
    w_down = noise(splits[4], (FF, D), FF ** -0.5, 0.109375, ((0, 2),))
    ln1_gain = jnp.clip(1.0 + 0.1 * jax.random.normal(splits[5], (D,), jnp.float32), 0.5, 1.5).astype(jnp.bfloat16)
    ln1_bias = noise(splits[6], (D,), 0.2, 3.0, ((0, 2),))
    q_bias = noise(splits[7], (D,), 0.3, 4.0, ((0, 2),))
    v_bias = noise(splits[8], (D,), 0.05, 0.75, ((0, 2),))
    out_bias = noise(splits[9], (D,), 0.3, 4.0, ((0, 2),))
    ln2_gain = jnp.clip(1.0 + 0.1 * jax.random.normal(splits[10], (D,), jnp.float32), 0.5, 1.5).astype(jnp.bfloat16)
    ln2_bias = noise(splits[11], (D,), 0.2, 3.0, ((0, 2),))
    up_bias = noise(splits[12], (FF,), 0.5, 6.0, ((0, 2),))
    down_bias = noise(splits[13], (D,), 0.3, 4.0, ((0, 2),))
    cotangent = noise(splits[14], (BATCH, LEN, D), 1.0, 6.0, ((0, 4), (1, 8)))
    return dict(inputs=inputs, w_qkv=w_qkv, w_out=w_out, w_up=w_up, w_down=w_down, ln1_gain=ln1_gain, ln1_bias=ln1_bias, q_bias=q_bias, v_bias=v_bias, out_bias=out_bias, ln2_gain=ln2_gain, ln2_bias=ln2_bias, up_bias=up_bias, down_bias=down_bias, cotangent=cotangent)


@jax.custom_vjp
def low(v):
    return lax.optimization_barrier(v.astype(jnp.bfloat16)).astype(jnp.float32)

@jax.custom_vjp
def low_back(v):
    return v

def low_keep(v):
    return (low(v), None)

def low_pass(kept, grad):
    return (grad,)

def back_keep(v):
    return (v, None)

def back_low(kept, grad):
    return (low(grad),)
low.defvjp(low_keep, low_pass)
low_back.defvjp(back_keep, back_low)
norm_eps = 1e-05
masked_fill = -1e+30

def matmul_high(left, right):
    return jnp.dot(left, right, precision=lax.Precision.HIGHEST)

def layer_norm(values, gain, shift):
    average = lax.optimization_barrier(jnp.mean(values, axis=-1, keepdims=True))
    centred = values - average
    spread = lax.optimization_barrier(jnp.mean(centred * centred, axis=-1, keepdims=True))
    return centred * lax.rsqrt(spread + norm_eps) * gain + shift

def exact_gelu(values):
    return jax.nn.gelu(values, approximate=False)

def attend_rows(keys, values, pair):
    start, queries = pair
    scores = low_back(jnp.einsum('qhe,khe->hqk', queries, keys, precision=lax.Precision.HIGHEST))
    rows = start + jnp.arange(queries.shape[0], dtype=jnp.int32)
    columns = jnp.arange(keys.shape[0], dtype=jnp.int32)
    allowed = (columns[None, :] <= rows[:, None])[None]
    scores = jnp.where(allowed, scores, masked_fill)
    highest = lax.optimization_barrier(jnp.max(scores, axis=-1, keepdims=True))
    weights = jnp.exp(scores - highest)
    weights = weights / lax.optimization_barrier(jnp.sum(weights, axis=-1, keepdims=True))
    weights = low(weights)
    return jnp.einsum('hqk,khe->qhe', weights, values, precision=lax.Precision.HIGHEST)

def block_forward(sequence, params):
    w_qkv, w_out, w_up, w_down, ln1_gain, ln1_bias, q_bias, v_bias, out_bias, ln2_gain, ln2_bias, up_bias, down_bias = params
    length = sequence.shape[0]
    normed1 = low(layer_norm(sequence, ln1_gain, ln1_bias))
    projected = matmul_high(normed1, w_qkv)
    queries = low(low_back((projected[:, :D] + q_bias) * HD ** (-0.5)))
    keys = low(low_back(projected[:, D:2 * D]))
    values = low(low_back(projected[:, 2 * D:] + v_bias))
    step = math.gcd(length, 512)
    starts = jnp.arange(0, length, step, dtype=jnp.int32)
    query_blocks = queries.reshape(length // step, step, H, HD)
    attend = jax.checkpoint(partial(attend_rows, keys.reshape(length, H, HD), values.reshape(length, H, HD)))
    attended = lax.map(attend, (starts, query_blocks)).reshape(length, D)
    attended = low(low_back(attended))
    branch = low_back(matmul_high(attended, w_out) + out_bias)
    middle = sequence + branch
    normed2 = low(layer_norm(middle, ln2_gain, ln2_bias))
    hidden = low_back(matmul_high(normed2, w_up) + up_bias)
    activated = low(exact_gelu(hidden))
    return middle + matmul_high(activated, w_down) + down_bias

def reference(inputs, w_qkv, w_out, w_up, w_down, ln1_gain, ln1_bias, q_bias, v_bias, out_bias, ln2_gain, ln2_bias, up_bias, down_bias, cotangent):
    params = tuple((param.astype(jnp.float32) for param in (w_qkv, w_out, w_up, w_down, ln1_gain, ln1_bias, q_bias, v_bias, out_bias, ln2_gain, ln2_bias, up_bias, down_bias)))

    def one_sequence(totals, pair):
        sequence, seq_cot = pair
        result, pullback = jax.vjp(block_forward, sequence.astype(jnp.float32), params)
        grad_input, grad_params = pullback(seq_cot.astype(jnp.float32))
        totals = jax.tree.map(jnp.add, totals, grad_params)
        return (totals, (result.astype(jnp.bfloat16), grad_input.astype(jnp.bfloat16)))
    zeros = jax.tree.map(jnp.zeros_like, params)
    totals, (outputs, input_grads) = lax.scan(one_sequence, zeros, (inputs, cotangent))
    return (outputs, input_grads, totals[0], totals[1], totals[2], totals[3], totals[4], totals[5], totals[6], totals[7], totals[8], totals[9], totals[10], totals[11], totals[12])
```

```python
import math

import jax
import jax.numpy as jnp
from jax import lax
from jax.experimental import pallas as pl
from jax.experimental.pallas import tpu as pltpu
from jax.sharding import PartitionSpec as P

H = 12
HD = 64
F32 = jnp.float32
BF16 = jnp.bfloat16

norm_eps = 1e-05
masked_fill = -1e30
ROWS = 256
VMEM_LIMIT = 56 * 1024 * 1024


def layer_norm(values, gain, shift):
    average = jnp.mean(values, axis=-1, keepdims=True)
    centred = values - average
    spread = jnp.mean(centred * centred, axis=-1, keepdims=True)
    return centred * lax.rsqrt(spread + norm_eps) * gain + shift


def exact_gelu(values):
    return jax.nn.gelu(values, approximate=False)


def dot_nt(left, right):
    return lax.dot_general(left, right, (((1,), (1,)), ((), ())), preferred_element_type=F32)


def dot_tn(left, right):
    return lax.dot_general(left, right, (((0,), (0,)), ((), ())), preferred_element_type=F32)


def diagonal_mask(rows):
    keys = lax.broadcasted_iota(jnp.int32, (rows, rows), 0)
    queries = lax.broadcasted_iota(jnp.int32, (rows, rows), 1)
    return keys <= queries


def forward_kernel(q_ref, k_ref, v_ref, o_ref, log_ref):
    length = q_ref.shape[1]
    rows = math.gcd(length, ROWS)
    allowed = diagonal_mask(rows)
    for i in range(length // rows):
        here = pl.ds(i * rows, rows)
        queries = q_ref[0, here, :]
        near = jnp.where(allowed, dot_nt(k_ref[0, here, :], queries), masked_fill)
        high = jnp.max(near, axis=0, keepdims=True)
        if i:
            before = pl.ds(0, i * rows)
            far = dot_nt(k_ref[0, before, :], queries)
            high = jnp.maximum(high, jnp.max(far, axis=0, keepdims=True))
        near = jnp.exp(near - high)
        total = jnp.sum(near, axis=0, keepdims=True)
        accum = dot_tn(v_ref[0, here, :], near.astype(BF16))
        if i:
            far = jnp.exp(far - high)
            total = total + jnp.sum(far, axis=0, keepdims=True)
            accum = accum + dot_tn(v_ref[0, before, :], far.astype(BF16))
        o_ref[0, here, :] = (accum / total).T.astype(BF16)
        log_ref[0, :, here] = high + jnp.log(total)


def backward_kernel(
    q_ref, k_ref, v_ref, o_ref, log_ref, up_ref, dq_ref, dk_ref, dv_ref, dk_sum, dv_sum
):
    length = q_ref.shape[1]
    rows = math.gcd(length, ROWS)
    allowed = diagonal_mask(rows)
    for i in reversed(range(length // rows)):
        here = pl.ds(i * rows, rows)
        queries = q_ref[0, here, :]
        upstream = up_ref[0, here, :]
        log_total = log_ref[0, :, here]
        mixed = upstream.astype(F32) * o_ref[0, here, :].astype(F32)
        delta = jnp.sum(mixed.T, axis=0, keepdims=True)
        first = i == length // rows - 1

        def part(where, masked):
            keys = k_ref[0, where, :]
            probs = jnp.exp(dot_nt(keys, queries) - log_total)
            if masked:
                probs = jnp.where(allowed, probs, 0.0)
            prob_grad = dot_nt(v_ref[0, where, :], upstream)
            score_low = (probs * (prob_grad - delta)).astype(BF16)
            dk_part = jnp.dot(score_low, queries, preferred_element_type=F32)
            dv_part = jnp.dot(probs.astype(BF16), upstream, preferred_element_type=F32)
            if first:
                dk_sum[where, :] = dk_part
                dv_sum[where, :] = dv_part
            else:
                dk_sum[where, :] += dk_part
                dv_sum[where, :] += dv_part
            return dot_tn(keys, score_low)

        dq = part(here, True)
        if i:
            dq = dq + part(pl.ds(0, i * rows), False)
        dq_ref[0, here, :] = dq.T.astype(BF16)
    dk_ref[0] = dk_sum[...].astype(BF16)
    dv_ref[0] = dv_sum[...].astype(BF16)


def head_block(length):
    return pl.BlockSpec((1, length, HD), lambda h: (h, 0, 0))


def row_block(length):
    return pl.BlockSpec((1, 1, length), lambda h: (h, 0, 0))


def attend_forward(queries, keys, values):
    heads, length, _ = queries.shape
    pairs = heads * length * length // 2
    return pl.pallas_call(
        forward_kernel,
        grid=(heads,),
        in_specs=[head_block(length)] * 3,
        out_specs=[head_block(length), row_block(length)],
        out_shape=[
            jax.ShapeDtypeStruct((heads, length, HD), BF16),
            jax.ShapeDtypeStruct((heads, 1, length), F32),
        ],
        compiler_params=pltpu.CompilerParams(vmem_limit_bytes=VMEM_LIMIT),
        cost_estimate=pl.CostEstimate(
            flops=16 * pairs * HD, bytes_accessed=8 * heads * length * HD, transcendentals=pairs
        ),
    )(queries, keys, values)


def attend_backward(queries, keys, values, attended, log_total, upstream):
    heads, length, _ = queries.shape
    pairs = heads * length * length // 2
    return pl.pallas_call(
        backward_kernel,
        grid=(heads,),
        in_specs=[head_block(length)] * 4 + [row_block(length), head_block(length)],
        out_specs=[head_block(length)] * 3,
        out_shape=[jax.ShapeDtypeStruct((heads, length, HD), BF16)] * 3,
        scratch_shapes=[pltpu.VMEM((length, HD), F32)] * 2,
        compiler_params=pltpu.CompilerParams(vmem_limit_bytes=VMEM_LIMIT),
        cost_estimate=pl.CostEstimate(
            flops=40 * pairs * HD, bytes_accessed=16 * heads * length * HD, transcendentals=pairs
        ),
    )(queries, keys, values, attended, log_total, upstream)


def to_heads(arrays):
    seqs, block, width = arrays[0].shape
    members = lax.axis_size("ctx")
    group = members // seqs
    held = -(-H // group)
    count = len(arrays)
    stacked = jnp.stack(arrays)
    padded = group * held * HD
    if padded > width:
        stacked = jnp.pad(stacked, ((0, 0), (0, 0), (0, 0), (0, padded - width)))
    stacked = stacked.reshape(count, seqs, block, group, held * HD)
    stacked = stacked.transpose(1, 3, 2, 0, 4).reshape(members, block, count * held * HD)
    moved = lax.all_to_all(stacked, "ctx", 0, 0)
    moved = moved.reshape(members * block, count, held, HD).transpose(1, 2, 0, 3)
    return [moved[i] for i in range(count)]


def to_tokens(arrays, seqs, block, width):
    members = lax.axis_size("ctx")
    group = members // seqs
    held = arrays[0].shape[0]
    count = len(arrays)
    stacked = jnp.stack(arrays).transpose(2, 0, 1, 3).reshape(members, block, count * held * HD)
    moved = lax.all_to_all(stacked, "ctx", 0, 0)
    moved = moved.reshape(seqs, group, block, count, held * HD).transpose(3, 0, 2, 1, 4)
    moved = moved.reshape(count, seqs * block, group * held * HD)[:, :, :width]
    return [moved[i] for i in range(count)]


def across(value, axis, bit):
    size = lax.axis_size(axis)
    return lax.ppermute(value, axis, [(i, i ^ bit) for i in range(size)])


def halves(pair, axis, bit, dim):
    side = (lax.axis_index(axis) // bit) % 2
    kept = lax.dynamic_index_in_dim(pair, side, dim, keepdims=False)
    given = lax.dynamic_index_in_dim(pair, 1 - side, dim, keepdims=False)
    return (kept.astype(F32) + across(given, axis, bit).astype(F32)).astype(BF16)


def doubled(part, axis, bit):
    side = (lax.axis_index(axis) // bit) % 2
    other = across(part, axis, bit)
    low = jnp.where(side == 0, part, other)
    high = jnp.where(side == 0, other, part)
    return jnp.concatenate([low, high], axis=0)


def bits_of(axis, first):
    bits = []
    while first < lax.axis_size(axis):
        bits.append((axis, first))
        first *= 2
    return bits


def sum_shares(grad):
    width = grad.shape[1]
    stages = bits_of("dp", 1) + bits_of("ctx", 2)
    part = halves(grad.astype(BF16).reshape(2, 2, -1, width), "ctx", 1, 1)
    part = halves(part, "fsdp", 1, 0)
    for axis, bit in stages:
        part = halves(part.reshape(2, -1, width), axis, bit, 0)
    for axis, bit in reversed(stages):
        part = doubled(part, axis, bit)
    return doubled(part, "ctx", 1).astype(F32)


def gather_weight(shard):
    rows, width = shard.shape
    side = lax.axis_index("ctx") % 2
    mine = lax.dynamic_index_in_dim(shard.reshape(2, rows // 2, width), side, 0, keepdims=False)
    theirs = doubled(across(mine, "fsdp", 1), "ctx", 1)
    place = lax.axis_index("fsdp")
    low = jnp.where(place == 0, shard, theirs)
    high = jnp.where(place == 0, theirs, shard)
    return jnp.concatenate([low, high], axis=0)


def per_device(
    inputs,
    w_qkv,
    w_out,
    w_up,
    w_down,
    ln1_gain,
    ln1_bias,
    q_bias,
    v_bias,
    out_bias,
    ln2_gain,
    ln2_bias,
    up_bias,
    down_bias,
    cotangent,
):
    qkv_full = gather_weight(w_qkv)
    out_full = lax.all_gather(w_out, "fsdp", axis=0, tiled=True)
    up_full = lax.all_gather(w_up, "fsdp", axis=0, tiled=True)
    down_full = lax.all_gather(w_down, "fsdp", axis=0, tiled=True)
    short = [
        ln1_gain,
        ln1_bias,
        q_bias,
        v_bias,
        out_bias,
        ln2_gain,
        ln2_bias,
        down_bias,
    ]
    piece = ln1_gain.shape[0]
    packed = jnp.concatenate(short + [up_bias]).reshape(1, -1)
    packed = lax.all_gather(packed, "fsdp", axis=0, tiled=True)
    (
        gain_one,
        shift_one,
        query_shift,
        value_shift,
        branch_shift,
        gain_two,
        shift_two,
        final_shift,
    ) = [packed[:, i * piece : (i + 1) * piece].reshape(-1) for i in range(len(short))]
    hidden_shift = packed[:, len(short) * piece :].reshape(-1)
    seqs, block, width = inputs.shape
    tokens = seqs * block
    scale = HD ** (-0.5)
    flat_in = inputs.reshape(tokens, width).astype(jnp.float32)
    normed1, norm1_pull = jax.vjp(
        layer_norm, flat_in, gain_one.astype(jnp.float32), shift_one.astype(jnp.float32)
    )
    normed1_low = normed1.astype(jnp.bfloat16)
    projected = jnp.dot(normed1_low, qkv_full, preferred_element_type=jnp.float32)
    queries = (
        ((projected[:, :width] + query_shift.astype(jnp.float32)) * scale)
        .astype(jnp.bfloat16)
        .reshape(seqs, block, width)
    )
    keys = projected[:, width : 2 * width].astype(jnp.bfloat16).reshape(seqs, block, width)
    values = (
        (projected[:, 2 * width :] + value_shift.astype(jnp.float32))
        .astype(jnp.bfloat16)
        .reshape(seqs, block, width)
    )
    heads_q, heads_k, heads_v = to_heads([queries, keys, values])
    heads_o, log_total = attend_forward(heads_q, heads_k, heads_v)
    (attended_low,) = to_tokens([heads_o], seqs, block, width)
    middle = (
        flat_in
        + jnp.dot(attended_low, out_full, preferred_element_type=jnp.float32)
        + branch_shift.astype(jnp.float32)
    )
    normed2, norm2_pull = jax.vjp(
        layer_norm, middle, gain_two.astype(jnp.float32), shift_two.astype(jnp.float32)
    )
    normed2_low = normed2.astype(jnp.bfloat16)
    hidden = jnp.dot(
        normed2_low, up_full, preferred_element_type=jnp.float32
    ) + hidden_shift.astype(jnp.float32)
    activated, gelu_pull = jax.vjp(exact_gelu, hidden)
    activated_low = activated.astype(jnp.bfloat16)
    output = (
        middle
        + jnp.dot(activated_low, down_full, preferred_element_type=jnp.float32)
        + final_shift.astype(jnp.float32)
    )
    result = output.astype(jnp.bfloat16).reshape(seqs, block, width)
    upstream_low = cotangent.reshape(tokens, width)
    upstream = upstream_low.astype(jnp.float32)
    down_grad = jnp.einsum(
        "rf,rd->fd", activated_low, upstream_low, preferred_element_type=jnp.float32
    )
    final_shift_grad = jnp.sum(upstream, axis=0)
    activated_grad = jnp.einsum(
        "rd,fd->rf", upstream_low, down_full, preferred_element_type=jnp.float32
    )
    hidden_low = gelu_pull(activated_grad)[0].astype(jnp.bfloat16)
    up_grad = jnp.einsum("rd,rf->df", normed2_low, hidden_low, preferred_element_type=jnp.float32)
    hidden_shift_grad = jnp.sum(hidden_low.astype(jnp.float32), axis=0)
    normed2_grad = jnp.einsum("rf,df->rd", hidden_low, up_full, preferred_element_type=jnp.float32)
    middle_part, gain_two_grad, shift_two_grad = norm2_pull(normed2_grad)
    middle_grad = upstream + middle_part
    branch_low = middle_grad.astype(jnp.bfloat16)
    branch_shift_grad = jnp.sum(branch_low.astype(jnp.float32), axis=0)
    out_grad = jnp.einsum("rd,re->de", attended_low, branch_low, preferred_element_type=jnp.float32)
    attended_grad = (
        jnp.einsum("re,de->rd", branch_low, out_full, preferred_element_type=jnp.float32)
        .astype(jnp.bfloat16)
        .reshape(seqs, block, width)
    )
    share_down = sum_shares(down_grad)
    share_up = sum_shares(up_grad)
    share_out = sum_shares(out_grad)
    (heads_up,) = to_heads([attended_grad])
    query_acc, key_acc, value_acc = to_tokens(
        attend_backward(heads_q, heads_k, heads_v, heads_o, log_total, heads_up),
        seqs,
        block,
        width,
    )
    query_pre = (query_acc.astype(F32) * scale).astype(BF16)
    key_low, value_low = key_acc, value_acc
    stacked = jnp.concatenate([query_pre, key_low, value_low], axis=1)
    qkv_grad = jnp.einsum("rd,rf->df", normed1_low, stacked, preferred_element_type=jnp.float32)
    query_shift_grad = jnp.sum(query_pre.astype(jnp.float32), axis=0)
    value_shift_grad = jnp.sum(value_low.astype(jnp.float32), axis=0)
    normed1_grad = jnp.einsum("rf,df->rd", stacked, qkv_full, preferred_element_type=jnp.float32)
    input_part, gain_one_grad, shift_one_grad = norm1_pull(normed1_grad)
    input_grad = (middle_grad + input_part).astype(jnp.bfloat16).reshape(seqs, block, width)
    share_qkv = sum_shares(qkv_grad)
    shards = lax.axis_size("fsdp")
    row_grads = [
        gain_one_grad,
        shift_one_grad,
        query_shift_grad,
        value_shift_grad,
        branch_shift_grad,
        gain_two_grad,
        shift_two_grad,
        final_shift_grad,
        hidden_shift_grad,
    ]
    rows = jnp.concatenate([grad.reshape(shards, -1) for grad in row_grads], axis=1)
    rows = lax.psum(rows, ("dp", "ctx", "fsdp"))
    mine = lax.dynamic_index_in_dim(rows, lax.axis_index("fsdp"), 0, keepdims=False)
    parts = [mine[i * piece : (i + 1) * piece] for i in range(8)]
    return (
        result,
        input_grad,
        share_qkv,
        share_out,
        share_up,
        share_down,
        *parts[:7],
        mine[8 * piece :],
        parts[7],
    )


def solution(mesh):
    return jax.shard_map(
        per_device,
        mesh=mesh,
        in_specs=(
            P(("dp", "fsdp"), "ctx", None),
            P("fsdp", None),
            P("fsdp", None),
            P("fsdp", None),
            P("fsdp", None),
            P("fsdp"),
            P("fsdp"),
            P("fsdp"),
            P("fsdp"),
            P("fsdp"),
            P("fsdp"),
            P("fsdp"),
            P("fsdp"),
            P("fsdp"),
            P(("dp", "fsdp"), "ctx", None),
        ),
        out_specs=(
            P(("dp", "fsdp"), "ctx", None),
            P(("dp", "fsdp"), "ctx", None),
            P("fsdp", None),
            P("fsdp", None),
            P("fsdp", None),
            P("fsdp", None),
            P("fsdp"),
            P("fsdp"),
            P("fsdp"),
            P("fsdp"),
            P("fsdp"),
            P("fsdp"),
            P("fsdp"),
            P("fsdp"),
            P("fsdp"),
        ),
        check_vma=False,
    )
```

```python
import math

import jax
import jax.numpy as jnp
from jax import lax
from jax.experimental import pallas as pl
from jax.experimental.pallas import tpu as pltpu
from jax.sharding import PartitionSpec as P

H = 12
HD = 64
F32 = jnp.float32
BF16 = jnp.bfloat16

norm_eps = 1e-05
masked_fill = -1e30
ROWS = 256
VMEM_LIMIT = 56 * 1024 * 1024


def layer_norm(values, gain, shift):
    average = jnp.mean(values, axis=-1, keepdims=True)
    centred = values - average
    spread = jnp.mean(centred * centred, axis=-1, keepdims=True)
    return centred * lax.rsqrt(spread + norm_eps) * gain + shift


def exact_gelu(values):
    return jax.nn.gelu(values, approximate=False)


def dot_nt(left, right):
    return lax.dot_general(left, right, (((1,), (1,)), ((), ())), preferred_element_type=F32)


def dot_tn(left, right):
    return lax.dot_general(left, right, (((0,), (0,)), ((), ())), preferred_element_type=F32)


def diagonal_mask(rows):
    keys = lax.broadcasted_iota(jnp.int32, (rows, rows), 0)
    queries = lax.broadcasted_iota(jnp.int32, (rows, rows), 1)
    return keys <= queries


def forward_kernel(q_ref, k_ref, v_ref, o_ref, log_ref):
    length = q_ref.shape[1]
    rows = math.gcd(length, ROWS)
    allowed = diagonal_mask(rows)
    for i in range(length // rows):
        here = pl.ds(i * rows, rows)
        queries = q_ref[0, here, :]
        near = jnp.where(allowed, dot_nt(k_ref[0, here, :], queries), masked_fill)
        high = jnp.max(near, axis=0, keepdims=True)
        if i:
            before = pl.ds(0, i * rows)
            far = dot_nt(k_ref[0, before, :], queries)
            high = jnp.maximum(high, jnp.max(far, axis=0, keepdims=True))
        near = jnp.exp(near - high)
        total = jnp.sum(near, axis=0, keepdims=True)
        accum = dot_tn(v_ref[0, here, :], near.astype(BF16))
        if i:
            far = jnp.exp(far - high)
            total = total + jnp.sum(far, axis=0, keepdims=True)
            accum = accum + dot_tn(v_ref[0, before, :], far.astype(BF16))
        o_ref[0, here, :] = (accum / total).T.astype(BF16)
        log_ref[0, :, here] = high + jnp.log(total)


def backward_kernel(
    q_ref, k_ref, v_ref, o_ref, log_ref, up_ref, dq_ref, dk_ref, dv_ref, dk_sum, dv_sum
):
    length = q_ref.shape[1]
    rows = math.gcd(length, ROWS)
    allowed = diagonal_mask(rows)
    for i in reversed(range(length // rows)):
        here = pl.ds(i * rows, rows)
        queries = q_ref[0, here, :]
        upstream = up_ref[0, here, :]
        log_total = log_ref[0, :, here]
        mixed = upstream.astype(F32) * o_ref[0, here, :].astype(F32)
        delta = jnp.sum(mixed.T, axis=0, keepdims=True)
        first = i == length // rows - 1

        def part(where, masked):
            keys = k_ref[0, where, :]
            probs = jnp.exp(dot_nt(keys, queries) - log_total)
            if masked:
                probs = jnp.where(allowed, probs, 0.0)
            prob_grad = dot_nt(v_ref[0, where, :], upstream)
            score_low = (probs * (prob_grad - delta)).astype(BF16)
            dk_part = jnp.dot(score_low, queries, preferred_element_type=F32)
            dv_part = jnp.dot(probs.astype(BF16), upstream, preferred_element_type=F32)
            if first:
                dk_sum[where, :] = dk_part
                dv_sum[where, :] = dv_part
            else:
                dk_sum[where, :] += dk_part
                dv_sum[where, :] += dv_part
            return dot_tn(keys, score_low)

        dq = part(here, True)
        if i:
            dq = dq + part(pl.ds(0, i * rows), False)
        dq_ref[0, here, :] = dq.T.astype(BF16)
    dk_ref[0] = dk_sum[...].astype(BF16)
    dv_ref[0] = dv_sum[...].astype(BF16)


def head_block(length):
    return pl.BlockSpec((1, length, HD), lambda h: (h, 0, 0))


def row_block(length):
    return pl.BlockSpec((1, 1, length), lambda h: (h, 0, 0))


def attend_forward(queries, keys, values):
    heads, length, _ = queries.shape
    pairs = heads * length * length // 2
    return pl.pallas_call(
        forward_kernel,
        grid=(heads,),
        in_specs=[head_block(length)] * 3,
        out_specs=[head_block(length), row_block(length)],
        out_shape=[
            jax.ShapeDtypeStruct((heads, length, HD), BF16),
            jax.ShapeDtypeStruct((heads, 1, length), F32),
        ],
        compiler_params=pltpu.CompilerParams(vmem_limit_bytes=VMEM_LIMIT),
        cost_estimate=pl.CostEstimate(
            flops=16 * pairs * HD, bytes_accessed=8 * heads * length * HD, transcendentals=pairs
        ),
    )(queries, keys, values)


def attend_backward(queries, keys, values, attended, log_total, upstream):
    heads, length, _ = queries.shape
    pairs = heads * length * length // 2
    return pl.pallas_call(
        backward_kernel,
        grid=(heads,),
        in_specs=[head_block(length)] * 4 + [row_block(length), head_block(length)],
        out_specs=[head_block(length)] * 3,
        out_shape=[jax.ShapeDtypeStruct((heads, length, HD), BF16)] * 3,
        scratch_shapes=[pltpu.VMEM((length, HD), F32)] * 2,
        compiler_params=pltpu.CompilerParams(vmem_limit_bytes=VMEM_LIMIT),
        cost_estimate=pl.CostEstimate(
            flops=40 * pairs * HD, bytes_accessed=16 * heads * length * HD, transcendentals=pairs
        ),
    )(queries, keys, values, attended, log_total, upstream)


def to_heads(arrays):
    seqs, block, width = arrays[0].shape
    members = lax.axis_size("ctx")
    group = members // seqs
    held = -(-H // group)
    count = len(arrays)
    stacked = jnp.stack(arrays)
    padded = group * held * HD
    if padded > width:
        stacked = jnp.pad(stacked, ((0, 0), (0, 0), (0, 0), (0, padded - width)))
    stacked = stacked.reshape(count, seqs, block, group, held * HD)
    stacked = stacked.transpose(1, 3, 2, 0, 4).reshape(members, block, count * held * HD)
    moved = lax.all_to_all(stacked, "ctx", 0, 0)
    moved = moved.reshape(members * block, count, held, HD).transpose(1, 2, 0, 3)
    return [moved[i] for i in range(count)]


def to_tokens(arrays, seqs, block, width):
    members = lax.axis_size("ctx")
    group = members // seqs
    held = arrays[0].shape[0]
    count = len(arrays)
    stacked = jnp.stack(arrays).transpose(2, 0, 1, 3).reshape(members, block, count * held * HD)
    moved = lax.all_to_all(stacked, "ctx", 0, 0)
    moved = moved.reshape(seqs, group, block, count, held * HD).transpose(3, 0, 2, 1, 4)
    moved = moved.reshape(count, seqs * block, group * held * HD)[:, :, :width]
    return [moved[i] for i in range(count)]


def across(value, axis, bit):
    size = lax.axis_size(axis)
    return lax.ppermute(value, axis, [(i, i ^ bit) for i in range(size)])


def halves(pair, axis, bit, dim):
    side = (lax.axis_index(axis) // bit) % 2
    kept = lax.dynamic_index_in_dim(pair, side, dim, keepdims=False)
    given = lax.dynamic_index_in_dim(pair, 1 - side, dim, keepdims=False)
    return (kept.astype(F32) + across(given, axis, bit).astype(F32)).astype(BF16)


def doubled(part, axis, bit):
    side = (lax.axis_index(axis) // bit) % 2
    other = across(part, axis, bit)
    low = jnp.where(side == 0, part, other)
    high = jnp.where(side == 0, other, part)
    return jnp.concatenate([low, high], axis=0)


def bits_of(axis, first):
    bits = []
    while first < lax.axis_size(axis):
        bits.append((axis, first))
        first *= 2
    return bits


def sum_shares(grad):
    width = grad.shape[1]
    stages = bits_of("dp", 1) + bits_of("ctx", 2)
    part = halves(grad.astype(BF16).reshape(2, 2, -1, width), "ctx", 1, 1)
    part = halves(part, "fsdp", 1, 0)
    for axis, bit in stages:
        part = halves(part.reshape(2, -1, width), axis, bit, 0)
    for axis, bit in reversed(stages):
        part = doubled(part, axis, bit)
    return doubled(part, "ctx", 1).astype(F32)


def sum_vectors(rows):
    place = lax.axis_index("fsdp")
    kept = lax.dynamic_index_in_dim(rows, place, 0, keepdims=True)
    given = lax.dynamic_index_in_dim(rows, 1 - place, 0, keepdims=True)
    part = kept + across(given, "fsdp", 1)
    for axis, bit in bits_of("ctx", 1) + bits_of("dp", 1):
        part = part + across(part, axis, bit)
    return part[0]


def gather_weight(shard):
    rows, width = shard.shape
    side = lax.axis_index("ctx") % 2
    mine = lax.dynamic_index_in_dim(shard.reshape(2, rows // 2, width), side, 0, keepdims=False)
    theirs = doubled(across(mine, "fsdp", 1), "ctx", 1)
    place = lax.axis_index("fsdp")
    low = jnp.where(place == 0, shard, theirs)
    high = jnp.where(place == 0, theirs, shard)
    return jnp.concatenate([low, high], axis=0)


def per_device(
    inputs,
    w_qkv,
    w_out,
    w_up,
    w_down,
    ln1_gain,
    ln1_bias,
    q_bias,
    v_bias,
    out_bias,
    ln2_gain,
    ln2_bias,
    up_bias,
    down_bias,
    cotangent,
):
    qkv_full = gather_weight(w_qkv)
    out_full = lax.all_gather(w_out, "fsdp", axis=0, tiled=True)
    up_full = lax.all_gather(w_up, "fsdp", axis=0, tiled=True)
    down_full = lax.all_gather(w_down, "fsdp", axis=0, tiled=True)
    short = [
        ln1_gain,
        ln1_bias,
        q_bias,
        v_bias,
        out_bias,
        ln2_gain,
        ln2_bias,
        down_bias,
    ]
    piece = ln1_gain.shape[0]
    packed = doubled(jnp.concatenate(short + [up_bias]).reshape(1, -1), "fsdp", 1)
    (
        gain_one,
        shift_one,
        query_shift,
        value_shift,
        branch_shift,
        gain_two,
        shift_two,
        final_shift,
    ) = [packed[:, i * piece : (i + 1) * piece].reshape(-1) for i in range(len(short))]
    hidden_shift = packed[:, len(short) * piece :].reshape(-1)
    seqs, block, width = inputs.shape
    tokens = seqs * block
    scale = HD ** (-0.5)
    flat_in = inputs.reshape(tokens, width).astype(jnp.float32)
    normed1, norm1_pull = jax.vjp(
        layer_norm, flat_in, gain_one.astype(jnp.float32), shift_one.astype(jnp.float32)
    )
    normed1_low = normed1.astype(jnp.bfloat16)
    projected = jnp.dot(normed1_low, qkv_full, preferred_element_type=jnp.float32)
    queries = (
        ((projected[:, :width] + query_shift.astype(jnp.float32)) * scale)
        .astype(jnp.bfloat16)
        .reshape(seqs, block, width)
    )
    keys = projected[:, width : 2 * width].astype(jnp.bfloat16).reshape(seqs, block, width)
    values = (
        (projected[:, 2 * width :] + value_shift.astype(jnp.float32))
        .astype(jnp.bfloat16)
        .reshape(seqs, block, width)
    )
    heads_q, heads_k, heads_v = to_heads([queries, keys, values])
    heads_o, log_total = attend_forward(heads_q, heads_k, heads_v)
    (attended_low,) = to_tokens([heads_o], seqs, block, width)
    middle = (
        flat_in
        + jnp.dot(attended_low, out_full, preferred_element_type=jnp.float32)
        + branch_shift.astype(jnp.float32)
    )
    normed2, norm2_pull = jax.vjp(
        layer_norm, middle, gain_two.astype(jnp.float32), shift_two.astype(jnp.float32)
    )
    normed2_low = normed2.astype(jnp.bfloat16)
    hidden = jnp.dot(
        normed2_low, up_full, preferred_element_type=jnp.float32
    ) + hidden_shift.astype(jnp.float32)
    activated, gelu_pull = jax.vjp(exact_gelu, hidden)
    activated_low = activated.astype(jnp.bfloat16)
    output = (
        middle
        + jnp.dot(activated_low, down_full, preferred_element_type=jnp.float32)
        + final_shift.astype(jnp.float32)
    )
    result = output.astype(jnp.bfloat16).reshape(seqs, block, width)
    upstream_low = cotangent.reshape(tokens, width)
    upstream = upstream_low.astype(jnp.float32)
    down_grad = jnp.einsum(
        "rf,rd->fd", activated_low, upstream_low, preferred_element_type=jnp.float32
    )
    final_shift_grad = jnp.sum(upstream, axis=0)
    activated_grad = jnp.einsum(
        "rd,fd->rf", upstream_low, down_full, preferred_element_type=jnp.float32
    )
    hidden_low = gelu_pull(activated_grad)[0].astype(jnp.bfloat16)
    up_grad = jnp.einsum("rd,rf->df", normed2_low, hidden_low, preferred_element_type=jnp.float32)
    hidden_shift_grad = jnp.sum(hidden_low.astype(jnp.float32), axis=0)
    normed2_grad = jnp.einsum("rf,df->rd", hidden_low, up_full, preferred_element_type=jnp.float32)
    middle_part, gain_two_grad, shift_two_grad = norm2_pull(normed2_grad)
    middle_grad = upstream + middle_part
    branch_low = middle_grad.astype(jnp.bfloat16)
    branch_shift_grad = jnp.sum(branch_low.astype(jnp.float32), axis=0)
    out_grad = jnp.einsum("rd,re->de", attended_low, branch_low, preferred_element_type=jnp.float32)
    attended_grad = (
        jnp.einsum("re,de->rd", branch_low, out_full, preferred_element_type=jnp.float32)
        .astype(jnp.bfloat16)
        .reshape(seqs, block, width)
    )
    share_down = sum_shares(down_grad)
    share_up = sum_shares(up_grad)
    share_out = sum_shares(out_grad)
    (heads_up,) = to_heads([attended_grad])
    query_acc, key_acc, value_acc = to_tokens(
        attend_backward(heads_q, heads_k, heads_v, heads_o, log_total, heads_up),
        seqs,
        block,
        width,
    )
    query_pre = (query_acc.astype(F32) * scale).astype(BF16)
    key_low, value_low = key_acc, value_acc
    stacked = jnp.concatenate([query_pre, key_low, value_low], axis=1)
    qkv_grad = jnp.einsum("rd,rf->df", normed1_low, stacked, preferred_element_type=jnp.float32)
    query_shift_grad = jnp.sum(query_pre.astype(jnp.float32), axis=0)
    value_shift_grad = jnp.sum(value_low.astype(jnp.float32), axis=0)
    normed1_grad = jnp.einsum("rf,df->rd", stacked, qkv_full, preferred_element_type=jnp.float32)
    input_part, gain_one_grad, shift_one_grad = norm1_pull(normed1_grad)
    input_grad = (middle_grad + input_part).astype(jnp.bfloat16).reshape(seqs, block, width)
    share_qkv = sum_shares(qkv_grad)
    shards = lax.axis_size("fsdp")
    row_grads = [
        gain_one_grad,
        shift_one_grad,
        query_shift_grad,
        value_shift_grad,
        branch_shift_grad,
        gain_two_grad,
        shift_two_grad,
        final_shift_grad,
        hidden_shift_grad,
    ]
    rows = jnp.concatenate([grad.reshape(shards, -1) for grad in row_grads], axis=1)
    mine = sum_vectors(rows)
    parts = [mine[i * piece : (i + 1) * piece] for i in range(8)]
    return (
        result,
        input_grad,
        share_qkv,
        share_out,
        share_up,
        share_down,
        *parts[:7],
        mine[8 * piece :],
        parts[7],
    )


def solution(mesh):
    return jax.shard_map(
        per_device,
        mesh=mesh,
        in_specs=(
            P(("dp", "fsdp"), "ctx", None),
            P("fsdp", None),
            P("fsdp", None),
            P("fsdp", None),
            P("fsdp", None),
            P("fsdp"),
            P("fsdp"),
            P("fsdp"),
            P("fsdp"),
            P("fsdp"),
            P("fsdp"),
            P("fsdp"),
            P("fsdp"),
            P("fsdp"),
            P(("dp", "fsdp"), "ctx", None),
        ),
        out_specs=(
            P(("dp", "fsdp"), "ctx", None),
            P(("dp", "fsdp"), "ctx", None),
            P("fsdp", None),
            P("fsdp", None),
            P("fsdp", None),
            P("fsdp", None),
            P("fsdp"),
            P("fsdp"),
            P("fsdp"),
            P("fsdp"),
            P("fsdp"),
            P("fsdp"),
            P("fsdp"),
            P("fsdp"),
            P("fsdp"),
        ),
        check_vma=False,
    )
```
